256 devices in a mesh: dp: 32 (over y, z), mp: 8 (over x, core).
Axes of the slice: x: 4, y: 4, z: 8, core: 2. Of those that a mesh axis runs over, the one named last changes fastest.
Arguments:
- gradient: bfloat16 [32, 256, 28672], P('dp', None, 'mp'), may hold values from -6 to 6
- feedback: float32 [32, 256, 28672], P('dp', None, 'mp'), may hold values from -3 to 3
- warm_basis: float32 [32, 28672], P(None, 'mp'), may hold values from -6 to 6
Outputs:
- approx: bfloat16 [256, 28672], P(None, 'mp')
- new_feedback: float32 [32, 256, 28672], P('dp', None, 'mp')
The draws below stay inside these ranges and needn't reach their ends.
All inputs are finite; a program needn't handle non-finite values.
Results may differ from the reference program's by a relative error of at most 0.001.
Values sent between devices are 32-bit elements; how exact they have to be, the bound alone decides.
No kernel may reach another device: no remote copies, remote signals or barrier semaphores. Data moves between devices by JAX's collectives and lax.ppermute only.
A program may use at most 64 MiB of HBM per device.

```python
import jax
import jax.numpy as jnp
from jax import lax

COLS = 28672
ROWS = 256
RANK = 32
REPLICAS = 32
N_DP = 32


def spiked(entries, own_key, source, target, parts, factor):
    def block_of(dim):
        return (jnp.arange(entries.shape[dim]) // (entries.shape[dim] // parts)).reshape((-1,) + (1,) * (entries.ndim - 1 - dim))

    one_side = jax.random.permutation(own_key, parts)[block_of(target)]
    other_side = (block_of(target) + parts // 2) % parts
    return jnp.where((block_of(source) == one_side) | (block_of(source) == other_side), factor * entries, entries)


def block_levels(stream_key, shape, cuts, low, top_value):
    level, own = 1.0, jax.random.fold_in(stream_key, 6)
    for dim, blocks in cuts:
        heights = jnp.exp(jax.random.uniform(jax.random.fold_in(own, dim), (blocks,), jnp.float32, low / len(cuts), top_value / len(cuts)))
        level = level * jnp.repeat(heights, shape[dim] // blocks).reshape([-1 if axis == dim else 1 for axis in range(len(shape))])
    return level


def scatter_about(key, shape, scale, reach, cuts=(), dtype=jnp.bfloat16):
    level = block_levels(key, shape, cuts, -0.22, 0.18) if cuts else 1.0
    array = jax.random.normal(key, shape, jnp.float32) * scale * level
    return jnp.minimum(jnp.maximum(array, -reach), reach).astype(dtype)


def bell_draw_with(key, shape, spread, reach, shards, heavy, kind=jnp.bfloat16):
    values = spread * jax.random.normal(key, shape, jnp.float32)
    if shards:
        values = values * block_levels(key, shape, shards, -0.22, 0.18)
    return jnp.clip(spiked(values, jax.random.fold_in(key, 3), *heavy), -reach, reach).astype(kind)


def setup_inputs(seed: int = 0) -> dict:
    seeds = jax.random.split(jax.random.key(seed), 4)
    return {
        "gradient": bell_draw_with(seeds[0], (REPLICAS, ROWS, COLS), 1.0, 6.0, ((0, 32), (2, 8)), (0, 1, 32, 2.75)),
        "feedback": scatter_about(seeds[1], (REPLICAS, ROWS, COLS), 0.5, 3.0, ((0, 32), (2, 8)), jnp.float32),
        "warm_basis": scatter_about(seeds[2], (RANK, COLS), 1.0, 6.0, ((1, 8),), jnp.float32),
    }


def lower_solve(factor_low, right_side):
    solved = []
    for index in range(factor_low.shape[0]):
        current = right_side[index]
        if index > 0:
            current = current - jnp.dot(factor_low[index, :index], jnp.stack(solved), precision=lax.Precision.HIGHEST)
        solved.append(current / factor_low[index, index])
    return jnp.stack(solved)

def reference(gradient, feedback, warm_basis):
    merged = gradient.astype(jnp.float32) + feedback
    total = jnp.sum(merged, axis=0)
    projected = jnp.dot(warm_basis, total.T, precision=lax.Precision.HIGHEST)
    gram_sum = jnp.dot(projected, projected.T, precision=lax.Precision.HIGHEST)
    factor_low = jnp.linalg.cholesky(gram_sum)
    ortho_basis = lower_solve(factor_low, projected)
    factor = jnp.dot(ortho_basis, total, precision=lax.Precision.HIGHEST)
    approx = jnp.dot(ortho_basis.T, factor, precision=lax.Precision.HIGHEST)
    new_feedback = merged - approx[None] / N_DP
    return (approx.astype(jnp.bfloat16), new_feedback)
```

```python
import functools

import jax
import jax.numpy as jnp
from jax import lax
from jax.experimental import pallas as pl
from jax.experimental.pallas import tpu as pltpu
from jax.sharding import Mesh
from jax.sharding import PartitionSpec as P

VMEM_LIMIT = 24 * 1024 * 1024
F32 = jnp.float32
BF16 = jnp.bfloat16


def halves(value):
    high = value.astype(BF16)
    return high, (value - high.astype(F32)).astype(BF16)


def dot(a, b, ca, cb):
    return lax.dot_general(a, b, (((ca,), (cb,)), ((), ())), preferred_element_type=F32)


def project_kernel(gradient_ref, feedback_ref, basis_ref, merged_ref, projected_ref):
    merged = gradient_ref[...].astype(F32) + feedback_ref[...]
    merged_ref[...] = merged
    high, low = halves(merged)
    basis_high, basis_low = halves(basis_ref[...])
    rank = basis_high.shape[0]
    both = dot(jnp.concatenate([basis_high, basis_low], axis=0), high, 1, 1)
    term = both[:rank] + both[rank:] + dot(basis_high, low, 1, 1)

    @pl.when(pl.program_id(0) == 0)
    def _():
        projected_ref[...] = term

    @pl.when(pl.program_id(0) != 0)
    def _():
        projected_ref[...] += term


def project(gradient, feedback, basis, block):
    rows, cols = feedback.shape
    rank = basis.shape[0]
    return pl.pallas_call(
        project_kernel,
        grid=(cols // block,),
        in_specs=[
            pl.BlockSpec((rows, block), lambda i: (0, i)),
            pl.BlockSpec((rows, block), lambda i: (0, i)),
            pl.BlockSpec((rank, block), lambda i: (0, i)),
        ],
        out_specs=[
            pl.BlockSpec((rows, block), lambda i: (0, i)),
            pl.BlockSpec((rank, rows), lambda i: (0, 0)),
        ],
        out_shape=[
            jax.ShapeDtypeStruct((rows, cols), F32),
            jax.ShapeDtypeStruct((rank, rows), F32),
        ],
        compiler_params=pltpu.CompilerParams(vmem_limit_bytes=VMEM_LIMIT),
        name="project",
    )(gradient, feedback, basis)


def factor_kernel(projected_ref, merged_ref, *out_refs):
    high, low = halves(merged_ref[...])
    p_high, p_low = halves(projected_ref[...])
    rank = p_high.shape[0]
    both = dot(jnp.concatenate([p_high, p_low], axis=0), high, 1, 0)
    term = both[:rank] + both[rank:] + dot(p_high, low, 1, 0)
    depth = rank // len(out_refs)
    for k, out_ref in enumerate(out_refs):
        out_ref[...] = term[k * depth : (k + 1) * depth]


def partial_factor(projected, merged, pieces, block):
    rank, rows = projected.shape
    cols = merged.shape[1]
    depth = rank // pieces
    return pl.pallas_call(
        factor_kernel,
        grid=(cols // block,),
        in_specs=[
            pl.BlockSpec((rank, rows), lambda i: (0, 0)),
            pl.BlockSpec((rows, block), lambda i: (0, i)),
        ],
        out_specs=[pl.BlockSpec((depth, block), lambda i: (0, i))] * pieces,
        out_shape=[jax.ShapeDtypeStruct((depth, cols), F32)] * pieces,
        compiler_params=pltpu.CompilerParams(vmem_limit_bytes=VMEM_LIMIT),
        name="partial_factor",
    )(projected, merged)


def solve_kernel(projected_ref, out_ref):
    p = projected_ref[...]
    rank = p.shape[0]
    exact = functools.partial(
        lax.dot_general, precision=lax.Precision.HIGHEST, preferred_element_type=F32
    )
    gram = exact(p, p, (((1,), (1,)), ((), ())))
    eye = (
        lax.broadcasted_iota(jnp.int32, (rank, rank), 0)
        == lax.broadcasted_iota(jnp.int32, (rank, rank), 1)
    ).astype(F32)
    state = jnp.concatenate([gram, eye], axis=1)
    row_id = lax.broadcasted_iota(jnp.int32, (rank, 1), 0)
    inverse_pivots = jnp.zeros((rank, 1), F32)
    for k in range(rank):
        row = state[k : k + 1, :]
        inverse = 1.0 / state[k : k + 1, k : k + 1]
        inverse_pivots = jnp.where(row_id == k, inverse, inverse_pivots)
        if k + 1 < rank:
            multiplier = jnp.where(row_id > k, state[:, k : k + 1] * inverse, 0.0)
            state = state - multiplier * row
    unit = state[:, rank:]
    basis = exact(unit, p, (((1,), (0,)), ((), ()))) * inverse_pivots
    out_ref[...] = exact(unit, basis, (((0,), (0,)), ((), ())))


def solve(projected):
    return pl.pallas_call(
        solve_kernel,
        out_shape=jax.ShapeDtypeStruct(projected.shape, F32),
        name="solve",
    )(projected)


def rebuild_kernel(scale, basis_ref, merged_ref, *refs):
    *factor_refs, approx_ref, updated_ref = refs
    b_high, b_low = halves(basis_ref[...])
    f_high, f_low = halves(jnp.concatenate([r[...] for r in factor_refs], axis=0))
    left = jnp.concatenate([b_high, b_high, b_low], axis=0)
    right = jnp.concatenate([f_high, f_low, f_high], axis=0)
    approx = dot(left, right, 0, 0)
    approx_ref[...] = approx.astype(BF16)
    updated_ref[...] = merged_ref[...] - approx * scale


def rebuild(basis, merged, factors, replicas, block):
    rank, rows = basis.shape
    cols = merged.shape[1]
    depth = factors[0].shape[0]
    return pl.pallas_call(
        functools.partial(rebuild_kernel, 1.0 / replicas),
        grid=(cols // block,),
        in_specs=[
            pl.BlockSpec((rank, rows), lambda i: (0, 0)),
            pl.BlockSpec((rows, block), lambda i: (0, i)),
        ]
        + [pl.BlockSpec((depth, block), lambda i: (0, i))] * len(factors),
        out_specs=[pl.BlockSpec((rows, block), lambda i: (0, i))] * 2,
        out_shape=[
            jax.ShapeDtypeStruct((rows, cols), BF16),
            jax.ShapeDtypeStruct((rows, cols), F32),
        ],
        compiler_params=pltpu.CompilerParams(vmem_limit_bytes=VMEM_LIMIT),
        name="rebuild",
    )(basis, merged, *factors)


def rotate(x, axis, size, step):
    return lax.ppermute(x, axis, [(i, (i + step) % size) for i in range(size)])


def sum_over(x, axes, size):
    spread = jnp.broadcast_to(x[None], (size,) + x.shape)
    return jnp.sum(lax.all_to_all(spread, axes, 0, 0), axis=0)


def sum_everywhere(x, sizes):
    core = lax.axis_index("core")
    half = x.shape[0] // 2
    pair = x.reshape(2, half, x.shape[1])
    mine = lax.dynamic_index_in_dim(pair, core, 0, False)
    other = lax.dynamic_index_in_dim(pair, 1 - core, 0, False)
    mine = mine + rotate(other, "core", 2, 1)
    mine = sum_over(mine, ("y", "x"), sizes["y"] * sizes["x"])
    mine = sum_over(mine, "z", sizes["z"])
    other = rotate(mine, "core", 2, 1)
    return jnp.where(
        core == 0, jnp.concatenate([mine, other]), jnp.concatenate([other, mine])
    )


def local(sizes, gradient, feedback, warm_basis):
    y, z = sizes["y"], sizes["z"]
    merged, projected = project(gradient[0], feedback[0], warm_basis, 896)
    projected = sum_everywhere(projected, sizes)
    rank = projected.shape[0]
    depth = rank // y
    place = lax.axis_index("y")
    blocks = projected.reshape(y, depth, -1)
    ahead = jnp.concatenate(
        [lax.dynamic_index_in_dim(blocks, (place + k) % y, 0, False) for k in range(y)]
    )
    pieces = partial_factor(ahead, merged, y, 896)
    arrived = [rotate(pieces[k], "y", y, k) for k in range(1, y)]
    basis = solve(projected).reshape(y, depth, -1)
    mine = pieces[0] + sum(arrived[1:], arrived[0])
    cols = mine.shape[1]
    summed = jnp.sum(
        lax.all_to_all(mine.reshape(z, depth // z, cols), "z", 0, 0), axis=0
    )
    spread = jnp.broadcast_to(summed[None], (z,) + summed.shape)
    whole = lax.all_to_all(spread, "z", 0, 0).reshape(depth, cols)
    factors = [whole] + [rotate(whole, "y", y, k) for k in range(1, y)]
    behind = jnp.concatenate(
        [lax.dynamic_index_in_dim(basis, (place - k) % y, 0, False) for k in range(y)]
    )
    approx, updated = rebuild(behind, merged, factors, y * z, 896)
    return (approx, updated[None])


def solution(mesh):
    sizes = {"y": 4, "z": 8, "x": 4, "core": 2}
    inner = Mesh(mesh.devices.reshape(tuple(sizes.values())), tuple(sizes))
    dp, mp = ("y", "z"), ("x", "core")
    return jax.shard_map(
        functools.partial(local, sizes),
        mesh=inner,
        in_specs=(P(dp, None, mp), P(dp, None, mp), P(None, mp)),
        out_specs=(P(None, mp), P(dp, None, mp)),
        check_vma=False,
    )
```

```python
import functools

import jax
import jax.numpy as jnp
from jax import lax
from jax.experimental import pallas as pl
from jax.experimental.pallas import tpu as pltpu
from jax.sharding import Mesh
from jax.sharding import PartitionSpec as P
F32 = jnp.float32
BF16 = jnp.bfloat16
MiB = 1024 * 1024

def halves(value):
    high = value.astype(BF16)
    return high, (value - high.astype(F32)).astype(BF16)

def dot(a, b, ca, cb):
    return lax.dot_general(a, b, (((ca,), (cb,)), ((), ())), preferred_element_type=F32)

def spans(cuts):
    start = 0
    for size in cuts:
        yield pl.ds(start, size)
        start += size

def project_kernel(cuts, inner, core, gradient, feedback, basis, merged, mine, other, p_buf, g_buf, f_buf, b_buf, g_sem, f_sem, b_sem):
    rank = basis.shape[0]
    fetch_basis = pltpu.make_async_copy(basis, b_buf, b_sem)
    fetch_basis.start()
    fetch = []
    for i, part in enumerate(spans(cuts)):
        pair = (pltpu.make_async_copy(feedback.at[part], f_buf.at[part], f_sem.at[i]),
                pltpu.make_async_copy(gradient.at[part], g_buf.at[part], g_sem.at[i]))
        for c in pair: c.start()
        fetch.append(pair)
    fetch_basis.wait()
    w_high, w_low = halves(b_buf[...])
    stack = jnp.concatenate([w_high, w_low], axis=0)
    terms = []
    cols = merged.shape[1]
    for i, part in enumerate(spans(cuts)):
        for c in fetch[i]: c.wait()
        total = None
        for k in range(0, cols, inner):
            span = pl.ds(k, inner)
            value = g_buf[part, span].astype(F32) + f_buf[part, span]
            merged[part, span] = value
            high, low = halves(value)
            both = dot(high, stack[:, k : k + inner], 1, 1)
            term = both[:, :rank] + both[:, rank:] + dot(low, w_high[:, k : k + inner], 1, 1)
            total = term if total is None else total + term
        terms.append(total)
    p_buf[...] = jnp.concatenate(terms, axis=0).T
    half = rank // 2
    mine[...] = p_buf[pl.ds(pl.multiple_of(core[0] * half, 8), half)]
    other[...] = p_buf[pl.ds(pl.multiple_of((1 - core[0]) * half, 8), half)]

def project(core, gradient, feedback, basis, cuts, inner=512, limit=24):
    rows, cols = feedback.shape
    rank = basis.shape[0]
    hbm = [pltpu.with_memory_space_constraint(x, pltpu.HBM) for x in (gradient, feedback, basis)]
    count = len(cuts)
    return pl.pallas_call(
        functools.partial(project_kernel, cuts, inner),
        in_specs=[pl.BlockSpec(memory_space=pltpu.SMEM)] + [pl.BlockSpec(memory_space=pltpu.HBM)] * 3,
        out_specs=[pl.BlockSpec(memory_space=pltpu.VMEM)] * 3,
        out_shape=[pltpu.VMEM((rows, cols), F32)] + [pltpu.VMEM((rank // 2, rows), F32)] * 2,
        scratch_shapes=[
            pltpu.VMEM((rank, rows), F32),
            pltpu.VMEM((rows, cols), BF16), pltpu.VMEM((rows, cols), F32), pltpu.VMEM((rank, cols), F32),
            pltpu.SemaphoreType.DMA((count,)), pltpu.SemaphoreType.DMA((count,)), pltpu.SemaphoreType.DMA],
        compiler_params=pltpu.CompilerParams(vmem_limit_bytes=limit * MiB),
        name="project",
    )(core, *hbm)

def factor_kernel(chunk, place, projected, merged, *outs):
    rank, count = projected.shape[0], len(outs)
    depth = rank // count
    rows = [projected[pl.ds(pl.multiple_of(lax.rem(place[0] + k, count) * depth, 8), depth)] for k in range(count)]
    p_high, p_low = halves(jnp.concatenate(rows, axis=0))
    stack = jnp.concatenate([p_high, p_low], axis=0)
    for i in range(merged.shape[1] // chunk):
        part = pl.ds(i * chunk, chunk)
        high, low = halves(merged[:, part])
        both = dot(stack, high, 1, 0)
        term = both[:rank] + both[rank:] + dot(p_high, low, 1, 0)
        for k, out in enumerate(outs):
            if len(out.shape) == 3:
                out[:, 0, part] = term[k * depth : (k + 1) * depth]
            else:
                out[:, part] = term[k * depth : (k + 1) * depth]

def partial_factor(place, projected, merged, shapes, chunk=896, limit=16):
    merged = pltpu.with_memory_space_constraint(merged, pltpu.VMEM)
    return pl.pallas_call(
        functools.partial(factor_kernel, chunk),
        in_specs=[pl.BlockSpec(memory_space=pltpu.SMEM)] + [pl.BlockSpec(memory_space=pltpu.VMEM)] * 2,
        out_specs=[pl.BlockSpec(memory_space=pltpu.VMEM)] * len(shapes),
        out_shape=[jax.ShapeDtypeStruct(shape, F32) for shape in shapes],
        compiler_params=pltpu.CompilerParams(vmem_limit_bytes=limit * MiB),
        name="partial_factor",
    )(place, projected, merged)

def rebuild_kernel(scale, cuts, place, basis, merged, *refs):
    *factors, approx, updated, a_buf, u_buf, a_sem, u_sem = refs
    count = len(factors)
    depth = basis.shape[0] // count
    rows = [basis[pl.ds(pl.multiple_of(lax.rem(place[0] + count - k, count) * depth, 8), depth)] for k in range(count)]
    b_high, b_low = halves(jnp.concatenate(rows, axis=0))
    left = jnp.concatenate([b_high, b_high, b_low], axis=0).T
    f_high, f_low = halves(jnp.concatenate([f[...] for f in factors], axis=0))
    right = jnp.concatenate([f_high, f_low, f_high], axis=0)
    copies = []
    for i, part in enumerate(spans(cuts)):
        value = dot(left[part.start : part.start + part.size], right, 1, 0)
        a_buf[part] = value.astype(BF16)
        u_buf[part] = merged[part] - value * scale
        for c in (pltpu.make_async_copy(u_buf.at[part], updated.at[part], u_sem.at[i]),
                  pltpu.make_async_copy(a_buf.at[part], approx.at[part], a_sem.at[i])):
            c.start()
            copies.append(c)
    for c in copies: c.wait()

def rebuild(place, basis, merged, factors, replicas, cuts, limit=24):
    rows, cols = merged.shape
    count = len(cuts)
    merged = pltpu.with_memory_space_constraint(merged, pltpu.VMEM)
    return pl.pallas_call(
        functools.partial(rebuild_kernel, 1.0 / replicas, cuts),
        in_specs=[pl.BlockSpec(memory_space=pltpu.SMEM)] + [pl.BlockSpec(memory_space=pltpu.VMEM)] * (2 + len(factors)),
        out_specs=[pl.BlockSpec(memory_space=pltpu.HBM)] * 2,
        out_shape=[pltpu.HBM((rows, cols), BF16), pltpu.HBM((rows, cols), F32)],
        scratch_shapes=[pltpu.VMEM((rows, cols), BF16), pltpu.VMEM((rows, cols), F32),
                        pltpu.SemaphoreType.DMA((count,)), pltpu.SemaphoreType.DMA((count,))],
        compiler_params=pltpu.CompilerParams(vmem_limit_bytes=limit * MiB),
        name="rebuild",
    )(place, basis, merged, *factors)

def solve_kernel(projected_ref, out_ref):
    p = projected_ref[...]
    rank = p.shape[0]
    exact = functools.partial(lax.dot_general, precision=lax.Precision.HIGHEST, preferred_element_type=F32)
    gram = exact(p, p, (((1,), (1,)), ((), ())))
    eye = (lax.broadcasted_iota(jnp.int32, (rank, rank), 0) == lax.broadcasted_iota(jnp.int32, (rank, rank), 1)).astype(F32)
    state = jnp.concatenate([gram, eye], axis=1)
    row_id = lax.broadcasted_iota(jnp.int32, (rank, 1), 0)
    inverse_pivots = jnp.zeros((rank, 1), F32)
    for k in range(rank):
        row = state[k : k + 1, :]
        inverse = 1.0 / state[k : k + 1, k : k + 1]
        inverse_pivots = jnp.where(row_id == k, inverse, inverse_pivots)
        if k + 1 < rank:
            multiplier = jnp.where(row_id > k, state[:, k : k + 1] * inverse, 0.0)
            state = state - multiplier * row
    unit = state[:, rank:]
    basis = exact(unit, p, (((1,), (0,)), ((), ()))) * inverse_pivots
    out_ref[...] = exact(unit, basis, (((0,), (0,)), ((), ())))

def solve(projected):
    return pl.pallas_call(
        solve_kernel,
        out_shape=jax.ShapeDtypeStruct(projected.shape, F32),
        compiler_params=pltpu.CompilerParams(vmem_limit_bytes=4 * MiB),
        name="solve",
    )(projected)


def rotate(x, axis, size, step):
    return lax.ppermute(x, axis, [(i, (i + step) % size) for i in range(size)])


def spread(x, axes, size):
    return lax.all_to_all(jnp.broadcast_to(x[None], (size,) + x.shape), axes, 0, 0)


def added(stacked):
    return functools.reduce(jnp.add, [stacked[i] for i in range(stacked.shape[0])])


def sum_over(x, axes, size):
    return added(spread(x, axes, size))


def sum_around(x, axis, size):
    arrived = [rotate(x, axis, size, k) for k in range(1, size)]
    return functools.reduce(jnp.add, arrived, x)


def sum_everywhere(mine, other, sizes):
    mine = mine + rotate(other, "core", 2, 1)
    mine = sum_over(mine, "z", sizes["z"])
    mine = sum_over(mine, ("y", "x"), sizes["y"] * sizes["x"])
    return jnp.concatenate([mine, rotate(mine, "core", 2, 1)])


def sum_factor(pieces, sizes):
    y, z = sizes["y"], sizes["z"]
    depth, cols = pieces[0].shape
    arrived = [rotate(pieces[k], "y", y, k) for k in range(1, y)]
    mine = functools.reduce(jnp.add, arrived, pieces[0])
    arrived = lax.all_to_all(mine.reshape(z, depth // z, cols), "z", 0, 0)
    whole = spread(added(arrived), "z", z).reshape(depth, cols)
    return [whole] + [rotate(whole, "y", y, k) for k in range(1, y)]


def shapes_of(rank, cols, sizes):
    return [(rank // sizes["y"], cols)] * sizes["y"]


def local(sizes, gradient, feedback, warm_basis):
    replicas = sizes["y"] * sizes["z"]
    rank, cols = warm_basis.shape
    core = lax.axis_index("core").reshape(1)
    place = lax.axis_index("y").reshape(1)
    core, place = lax.optimization_barrier((core, place))
    merged, mine, other = project(core, gradient[0], feedback[0], warm_basis, (128, 128))
    projected = sum_everywhere(mine, other, sizes)
    pieces = partial_factor(place, projected, merged, shapes_of(rank, cols, sizes))
    basis = solve(projected)
    factors = sum_factor(pieces, sizes)
    approx, updated = rebuild(place, basis, merged, factors, replicas, (64, 64, 64, 64))
    return (approx, updated[None])


def solution(mesh):
    sizes = {"y": 4, "z": 8, "x": 4, "core": 2}
    inner = Mesh(mesh.devices.reshape(tuple(sizes.values())), tuple(sizes))
    dp, mp = ("y", "z"), ("x", "core")
    return jax.shard_map(
        functools.partial(local, sizes),
        mesh=inner,
        in_specs=(P(dp, None, mp), P(dp, None, mp), P(None, mp)),
        out_specs=(P(None, mp), P(dp, None, mp)),
        check_vma=False,
    )
```

```python
import functools

import jax
import jax.numpy as jnp
from jax import lax
from jax.experimental import pallas as pl
from jax.experimental.pallas import tpu as pltpu
from jax.sharding import Mesh
from jax.sharding import PartitionSpec as P

F32 = jnp.float32
BF16 = jnp.bfloat16
MiB = 1024 * 1024
VMEM = pl.BlockSpec(memory_space=pltpu.VMEM)
HBM = pl.BlockSpec(memory_space=pltpu.HBM)


def halves(value):
    high = value.astype(BF16)
    return high, (value - high.astype(F32)).astype(BF16)


def dot(a, b, ca, cb):
    return lax.dot_general(a, b, (((ca,), (cb,)), ((), ())), preferred_element_type=F32)


def params(limit):
    return pltpu.CompilerParams(vmem_limit_bytes=limit * MiB)


def spans(cuts):
    start = 0
    for size in cuts:
        yield pl.ds(start, size)
        start += size


def column_block(place, k, count, width):
    return pl.ds(pl.multiple_of(lax.rem(place + k, count) * width, 128), width)


def project_kernel(cuts, inner, gradient, feedback, basis, *refs):
    merged, mine, other, p_buf, g_buf, f_buf, b_buf, g_sem, f_sem, b_sem = refs
    core = lax.axis_index("core")
    rank, cols = basis.shape
    fetch_basis = pltpu.make_async_copy(basis, b_buf, b_sem)
    fetch_basis.start()
    fetch = []
    for i, part in enumerate(spans(cuts)):
        pair = (
            pltpu.make_async_copy(feedback.at[part], f_buf.at[part], f_sem.at[i]),
            pltpu.make_async_copy(gradient.at[part], g_buf.at[part], g_sem.at[i]),
        )
        for copy in pair:
            copy.start()
        fetch.append(pair)
    fetch_basis.wait()
    w_high, w_low = halves(b_buf[...])
    stack = jnp.concatenate([w_high, w_low], axis=0)
    terms = []
    for i, part in enumerate(spans(cuts)):
        for copy in fetch[i]:
            copy.wait()
        total = None
        for at in range(0, cols, inner):
            span = pl.ds(at, inner)
            value = g_buf[part, span].astype(F32) + f_buf[part, span]
            merged[part, span] = value
            high, low = halves(value)
            both = dot(high, stack[:, at : at + inner], 1, 1)
            term = both[:, :rank] + both[:, rank:]
            term = term + dot(low, w_high[:, at : at + inner], 1, 1)
            total = term if total is None else total + term
        terms.append(total)
    p_buf[...] = jnp.concatenate(terms, axis=0).T
    half = rank // 2
    mine[...] = p_buf[pl.ds(pl.multiple_of(core * half, 8), half)]
    other[...] = p_buf[pl.ds(pl.multiple_of((1 - core) * half, 8), half)]


def project(gradient, feedback, basis, cuts=(128, 128), inner=512):
    rows, cols = feedback.shape
    rank = basis.shape[0]
    arrays = [
        pltpu.with_memory_space_constraint(x, pltpu.HBM)
        for x in (gradient, feedback, basis)
    ]
    return pl.pallas_call(
        functools.partial(project_kernel, cuts, inner),
        in_specs=[HBM] * 3,
        out_specs=[VMEM] * 3,
        out_shape=[pltpu.VMEM((rows, cols), F32)]
        + [pltpu.VMEM((rank // 2, rows), F32)] * 2,
        scratch_shapes=[
            pltpu.VMEM((rank, rows), F32),
            pltpu.VMEM((rows, cols), BF16),
            pltpu.VMEM((rows, cols), F32),
            pltpu.VMEM((rank, cols), F32),
            pltpu.SemaphoreType.DMA((len(cuts),)),
            pltpu.SemaphoreType.DMA((len(cuts),)),
            pltpu.SemaphoreType.DMA,
        ],
        compiler_params=params(20),
        name="project",
    )(*arrays)


def factor_kernel(blocks, projected, merged, out):
    rank = projected.shape[0]
    count, depth, width = out.shape
    groups = count // blocks
    p_high, p_low = halves(projected[...])
    stack = jnp.concatenate([p_high, p_low], axis=0)
    for k in range(blocks):
        high, low = halves(merged[:, k * width : (k + 1) * width])
        both = dot(stack, high, 1, 0)
        term = both[:rank] + both[rank:] + dot(p_high, low, 1, 0)
        out[k * groups : (k + 1) * groups] = term.reshape(groups, depth, width)


def partial_factor(projected, merged, blocks, shape):
    merged = pltpu.with_memory_space_constraint(merged, pltpu.VMEM)
    return pl.pallas_call(
        functools.partial(factor_kernel, blocks),
        in_specs=[VMEM] * 2,
        out_specs=VMEM,
        out_shape=jax.ShapeDtypeStruct(shape, F32),
        compiler_params=params(8),
        name="partial_factor",
    )(projected, merged)


def rebuild_kernel(scale, ahead, count, basis, merged, *refs):
    factors = refs[: len(ahead)]
    approx, updated, a_buf, u_buf, a_sem, u_sem = refs[-6:]
    rank = basis.shape[0]
    width = factors[0].shape[-1]
    place = lax.axis_index("y")
    b_high, b_low = halves(basis[...])
    left = jnp.concatenate([b_high, b_high, b_low], axis=0).T
    copies = []
    for i, (k, factor) in enumerate(zip(ahead, factors)):
        f_high, f_low = halves(factor[...].reshape(rank, width))
        value = dot(left, jnp.concatenate([f_high, f_low, f_high], axis=0), 1, 0)
        part = column_block(place, k, count, width)
        a_buf[i] = value.astype(BF16)
        u_buf[i] = merged[:, part] - value * scale
        for copy in (
            pltpu.make_async_copy(u_buf.at[i], updated.at[:, part], u_sem.at[i]),
            pltpu.make_async_copy(a_buf.at[i], approx.at[:, part], a_sem.at[i]),
        ):
            copy.start()
            copies.append(copy)
    for copy in copies:
        copy.wait()


def rebuild(basis, merged, factors, ahead, count, replicas, earlier=()):
    rows, cols = merged.shape
    width = cols // count
    merged = pltpu.with_memory_space_constraint(merged, pltpu.VMEM)
    earlier = [pltpu.with_memory_space_constraint(x, pltpu.HBM) for x in earlier]
    first = 2 + len(factors)
    return pl.pallas_call(
        functools.partial(rebuild_kernel, 1.0 / replicas, ahead, count),
        in_specs=[VMEM] * (2 + len(factors)) + [HBM] * len(earlier),
        out_specs=[HBM] * 2,
        out_shape=[pltpu.HBM((rows, cols), BF16), pltpu.HBM((rows, cols), F32)],
        input_output_aliases={first + i: i for i in range(len(earlier))},
        scratch_shapes=[
            pltpu.VMEM((len(ahead), rows, width), BF16),
            pltpu.VMEM((len(ahead), rows, width), F32),
            pltpu.SemaphoreType.DMA((len(ahead),)),
            pltpu.SemaphoreType.DMA((len(ahead),)),
        ],
        compiler_params=params(20),
        name="rebuild",
    )(basis, merged, *factors, *earlier)


def solve_kernel(projected_ref, out_ref):
    p = projected_ref[...]
    rank = p.shape[0]
    exact = functools.partial(
        lax.dot_general, precision=lax.Precision.HIGHEST, preferred_element_type=F32
    )
    gram = exact(p, p, (((1,), (1,)), ((), ())))
    eye = (
        lax.broadcasted_iota(jnp.int32, (rank, rank), 0)
        == lax.broadcasted_iota(jnp.int32, (rank, rank), 1)
    ).astype(F32)
    state = jnp.concatenate([gram, eye], axis=1)
    row_id = lax.broadcasted_iota(jnp.int32, (rank, 1), 0)
    inverse_pivots = jnp.zeros((rank, 1), F32)
    for k in range(rank):
        row = state[k : k + 1, :]
        inverse = 1.0 / state[k : k + 1, k : k + 1]
        inverse_pivots = jnp.where(row_id == k, inverse, inverse_pivots)
        if k + 1 < rank:
            multiplier = jnp.where(row_id > k, state[:, k : k + 1] * inverse, 0.0)
            state = state - multiplier * row
    unit = state[:, rank:]
    basis = exact(unit, p, (((1,), (0,)), ((), ()))) * inverse_pivots
    out_ref[...] = exact(unit, basis, (((0,), (0,)), ((), ())))


def solve(projected):
    return pl.pallas_call(
        solve_kernel,
        out_shape=jax.ShapeDtypeStruct(projected.shape, F32),
        compiler_params=params(4),
        name="solve",
    )(projected)


def rotate(x, axis, size, step):
    return lax.ppermute(x, axis, [(i, (i + step) % size) for i in range(size)])


def spread(x, axes, size):
    return lax.all_to_all(jnp.broadcast_to(x[None], (size,) + x.shape), axes, 0, 0)


def added(stacked):
    return functools.reduce(jnp.add, [stacked[i] for i in range(stacked.shape[0])])


def local(sizes, gradient, feedback, warm_basis):
    y, z, x = sizes["y"], sizes["z"], sizes["x"]
    rank, cols = warm_basis.shape
    width = cols // y
    merged, mine, other = project(gradient[0], feedback[0], warm_basis)

    mine = mine + rotate(other, "core", 2, 1)
    mine = added(spread(mine, "z", z))
    mine = added(spread(mine, ("y", "x"), y * x))
    projected = jnp.concatenate([mine, rotate(mine, "core", 2, 1)])

    factor = partial_factor(projected, merged, y, (y * z, rank // z, width))
    summed = added(lax.all_to_all(factor, ("y", "z"), 0, 0))
    whole = spread(summed, "z", z)
    arrived = [rotate(whole, "y", y, y - k) for k in range(1, y)]
    basis = solve(projected)
    build = functools.partial(rebuild, basis, merged, count=y, replicas=y * z)
    outs = build([whole], (0,))
    approx, updated = build(arrived, (1, 2, 3), earlier=outs)
    return (approx, updated[None])


def solution(mesh):
    sizes = {"y": 4, "z": 8, "x": 4, "core": 2}
    inner = Mesh(mesh.devices.reshape(tuple(sizes.values())), tuple(sizes))
    dp, mp = ("y", "z"), ("x", "core")
    return jax.shard_map(
        functools.partial(local, sizes),
        mesh=inner,
        in_specs=(P(dp, None, mp), P(dp, None, mp), P(None, mp)),
        out_specs=(P(None, mp), P(dp, None, mp)),
        check_vma=False,
    )
```

```python
import functools

import jax
import jax.numpy as jnp
from jax import lax
from jax.experimental import pallas as pl
from jax.experimental.pallas import tpu as pltpu
from jax.sharding import Mesh
from jax.sharding import PartitionSpec as P

F32 = jnp.float32
BF16 = jnp.bfloat16
MiB = 1024 * 1024
VMEM = pl.BlockSpec(memory_space=pltpu.VMEM)
HBM = pl.BlockSpec(memory_space=pltpu.HBM)


def halves(value):
    high = value.astype(BF16)
    return high, (value - high.astype(F32)).astype(BF16)


def dot(a, b, ca, cb):
    return lax.dot_general(a, b, (((ca,), (cb,)), ((), ())), preferred_element_type=F32)


def params(limit):
    return pltpu.CompilerParams(vmem_limit_bytes=limit * MiB)


def spans(cuts):
    start = 0
    for size in cuts:
        yield pl.ds(start, size)
        start += size


def column_block(index, width):
    return pl.ds(pl.multiple_of(index * width, 128), width)


def project_kernel(cuts, inner, gradient, feedback, basis, *refs):
    merged, mine, other, p_buf, g_buf, f_buf, b_buf, g_sem, f_sem, b_sem = refs
    core = lax.axis_index("core")
    rank, cols = basis.shape
    fetch_basis = pltpu.make_async_copy(basis, b_buf, b_sem)
    fetch_basis.start()
    fetch = []
    for i, part in enumerate(spans(cuts)):
        pair = (
            pltpu.make_async_copy(feedback.at[part], f_buf.at[part], f_sem.at[i]),
            pltpu.make_async_copy(gradient.at[part], g_buf.at[part], g_sem.at[i]),
        )
        for copy in pair:
            copy.start()
        fetch.append(pair)
    fetch_basis.wait()
    w_high, w_low = halves(b_buf[...])
    stack = jnp.concatenate([w_high, w_low], axis=0)
    terms = []
    for i, part in enumerate(spans(cuts)):
        for copy in fetch[i]:
            copy.wait()
        total = None
        for at in range(0, cols, inner):
            span = pl.ds(at, inner)
            value = g_buf[part, span].astype(F32) + f_buf[part, span]
            merged[part, span] = value
            high, low = halves(value)
            both = dot(high, stack[:, at : at + inner], 1, 1)
            term = both[:, :rank] + both[:, rank:]
            term = term + dot(low, w_high[:, at : at + inner], 1, 1)
            total = term if total is None else total + term
        terms.append(total)
    p_buf[...] = jnp.concatenate(terms, axis=0).T
    half = rank // 2
    mine[...] = p_buf[pl.ds(pl.multiple_of(core * half, 8), half)]
    other[...] = p_buf[pl.ds(pl.multiple_of((1 - core) * half, 8), half)]


def project(gradient, feedback, basis, cuts=(128, 128), inner=512):
    rows, cols = feedback.shape
    rank = basis.shape[0]
    arrays = [
        pltpu.with_memory_space_constraint(x, pltpu.HBM)
        for x in (gradient, feedback, basis)
    ]
    return pl.pallas_call(
        functools.partial(project_kernel, cuts, inner),
        in_specs=[HBM] * 3,
        out_specs=[VMEM] * 3,
        out_shape=[pltpu.VMEM((rows, cols), F32)]
        + [pltpu.VMEM((rank // 2, rows), F32)] * 2,
        scratch_shapes=[
            pltpu.VMEM((rank, rows), F32),
            pltpu.VMEM((rows, cols), BF16),
            pltpu.VMEM((rows, cols), F32),
            pltpu.VMEM((rank, cols), F32),
            pltpu.SemaphoreType.DMA((len(cuts),)),
            pltpu.SemaphoreType.DMA((len(cuts),)),
            pltpu.SemaphoreType.DMA,
        ],
        compiler_params=params(20),
        name="project",
    )(*arrays)


def factor_kernel(blocks, projected, merged, out):
    rank = projected.shape[0]
    count, depth, width = out.shape
    groups = count // blocks
    p_high, p_low = halves(projected[...])
    stack = jnp.concatenate([p_high, p_low], axis=0)
    for k in range(blocks):
        high, low = halves(merged[:, k * width : (k + 1) * width])
        both = dot(stack, high, 1, 0)
        term = both[:rank] + both[rank:] + dot(p_high, low, 1, 0)
        out[k * groups : (k + 1) * groups] = term.reshape(groups, depth, width)


def partial_factor(projected, merged, blocks, shape):
    merged = pltpu.with_memory_space_constraint(merged, pltpu.VMEM)
    return pl.pallas_call(
        functools.partial(factor_kernel, blocks),
        in_specs=[VMEM] * 2,
        out_specs=VMEM,
        out_shape=jax.ShapeDtypeStruct(shape, F32),
        compiler_params=params(8),
        name="partial_factor",
    )(projected, merged)


def rebuild_kernel(scale, across, count, basis, merged, factor, *refs):
    approx, updated, a_buf, u_buf, a_sem, u_sem = refs[-6:]
    rank = basis.shape[1] // 3
    groups, _, width = factor.shape
    groups //= count
    place = lax.axis_index("yh")
    place = 1 - place if across else place
    left = basis[...]
    copies = []
    for i in range(count):
        f = factor[i * groups : (i + 1) * groups].reshape(rank, width)
        f_high, f_low = halves(f)
        value = dot(left, jnp.concatenate([f_high, f_low, f_high], axis=0), 1, 0)
        part = column_block(2 * place + i, width)
        a_buf[i] = value.astype(BF16)
        u_buf[i] = merged[:, part] - value * scale
        for copy in (
            pltpu.make_async_copy(u_buf.at[i], updated.at[:, part], u_sem.at[i]),
            pltpu.make_async_copy(a_buf.at[i], approx.at[:, part], a_sem.at[i]),
        ):
            copy.start()
            copies.append(copy)
    for copy in copies:
        copy.wait()


def rebuild(basis, merged, factor, across, replicas, earlier=()):
    rows, cols = merged.shape
    width = factor.shape[2]
    count = cols // width // 2
    merged = pltpu.with_memory_space_constraint(merged, pltpu.VMEM)
    earlier = [pltpu.with_memory_space_constraint(x, pltpu.HBM) for x in earlier]
    return pl.pallas_call(
        functools.partial(rebuild_kernel, 1.0 / replicas, across, count),
        in_specs=[VMEM] * 3 + [HBM] * len(earlier),
        out_specs=[HBM] * 2,
        out_shape=[pltpu.HBM((rows, cols), BF16), pltpu.HBM((rows, cols), F32)],
        input_output_aliases={3 + i: i for i in range(len(earlier))},
        scratch_shapes=[
            pltpu.VMEM((count, rows, width), BF16),
            pltpu.VMEM((count, rows, width), F32),
            pltpu.SemaphoreType.DMA((count,)),
            pltpu.SemaphoreType.DMA((count,)),
        ],
        compiler_params=params(20),
        name="rebuild",
    )(basis, merged, factor, *earlier)


def solve_kernel(w, projected_ref, out_ref):
    p = projected_ref[...]
    rank = p.shape[0]
    exact = functools.partial(
        lax.dot_general, precision=lax.Precision.HIGHEST, preferred_element_type=F32
    )
    gram = exact(p, p, (((1,), (1,)), ((), ())))
    eye = (
        lax.broadcasted_iota(jnp.int32, (rank, rank), 0)
        == lax.broadcasted_iota(jnp.int32, (rank, rank), 1)
    ).astype(F32)
    state = jnp.concatenate([gram, eye], axis=1)
    row_id = lax.broadcasted_iota(jnp.int32, (rank, 1), 0)
    inverse_pivots = jnp.zeros((rank, 2 * rank), F32)
    for k in range(0, rank, w):
        rows = [state[k + j : k + j + 1, :] for j in range(w)]
        cols = [jnp.broadcast_to(state[:, k + j : k + j + 1], state.shape) for j in range(w)]
        block = {(i, j): cols[j][k + i : k + i + 1, :] for i in range(w) for j in range(i + 1)}
        change = None
        inverse, ratio = [], {}
        for j in range(w):
            inverse.append(1.0 / block[j, j])
            for i in range(j + 1, w):
                ratio[i, j] = block[i, j] * inverse[j]
            for i in range(j + 1, w):
                for l in range(j + 1, i + 1):
                    block[i, l] = block[i, l] - ratio[i, j] * block[l, j]
        for j in range(w):
            for i in range(j + 1, w):
                rows[i] = rows[i] - ratio[i, j] * rows[j]
                cols[i] = cols[i] - ratio[i, j] * cols[j]
            inverse_pivots = jnp.where(row_id == k + j, inverse[j], inverse_pivots)
            if k + j + 1 < rank:
                term = jnp.where(row_id > k + j, cols[j] * inverse[j], 0.0) * rows[j]
                change = term if change is None else change + term
        if change is not None:
            state = state - change
    unit = state[:, rank:]
    basis = exact(unit, p, (((1,), (0,)), ((), ()))) * inverse_pivots[:, :1]
    high, low = halves(exact(unit, basis, (((0,), (0,)), ((), ()))))
    out_ref[...] = jnp.concatenate([high, high, low], axis=0).T


def solve(projected):
    return pl.pallas_call(
        functools.partial(solve_kernel, 8),
        out_shape=jax.ShapeDtypeStruct((projected.shape[1], 3 * projected.shape[0]), BF16),
        compiler_params=params(4),
        name="solve",
    )(projected)


def rotate(x, axis, size, step):
    return lax.ppermute(x, axis, [(i, (i + step) % size) for i in range(size)])


def mirror(x, size):
    pairs = [(i, size - 1 - i) for i in range(size)]
    return lax.ppermute(x, ("yh", "yl"), pairs)


def spread(x, axes, size):
    return lax.all_to_all(jnp.broadcast_to(x[None], (size,) + x.shape), axes, 0, 0)


def added(stacked):
    return functools.reduce(jnp.add, [stacked[i] for i in range(stacked.shape[0])])


def local(sizes, gradient, feedback, warm_basis):
    z, x = sizes["z"], sizes["x"]
    y = sizes["yh"] * sizes["yl"]
    rank, cols = warm_basis.shape
    width = cols // y
    merged, mine, other = project(gradient[0], feedback[0], warm_basis)

    mine = mine + rotate(other, "core", 2, 1)
    mine = added(spread(mine, "z", z))
    mine = added(spread(mine, ("yh", "yl", "x"), y * x))
    projected = jnp.concatenate([mine, rotate(mine, "core", 2, 1)])

    factor = partial_factor(projected, merged, y, (y * z, rank // z, width))
    summed = added(lax.all_to_all(factor, ("yh", "yl", "z"), 0, 0))
    here = spread(summed, ("yl", "z"), y // 2 * z)
    there = mirror(here, y)
    basis = solve(projected)
    build = functools.partial(rebuild, basis, merged, replicas=y * z)
    outs = build(here, False)
    approx, updated = build(there, True, earlier=outs)
    return (approx, updated[None])


def solution(mesh):
    sizes = {"yh": 2, "yl": 2, "z": 8, "x": 4, "core": 2}
    inner = Mesh(mesh.devices.reshape(tuple(sizes.values())), tuple(sizes))
    dp, mp = ("yh", "yl", "z"), ("x", "core")
    return jax.shard_map(
        functools.partial(local, sizes),
        mesh=inner,
        in_specs=(P(dp, None, mp), P(dp, None, mp), P(None, mp)),
        out_specs=(P(None, mp), P(dp, None, mp)),
        check_vma=False,
    )
```

```python
import functools

import jax
import jax.numpy as jnp
from jax import lax
from jax.experimental import pallas as pl
from jax.experimental.pallas import tpu as pltpu
from jax.sharding import Mesh
from jax.sharding import PartitionSpec as P

F32 = jnp.float32
BF16 = jnp.bfloat16
MiB = 1024 * 1024
VMEM = pl.BlockSpec(memory_space=pltpu.VMEM)
HBM = pl.BlockSpec(memory_space=pltpu.HBM)


def halves(value):
    high = value.astype(BF16)
    return high, (value - high.astype(F32)).astype(BF16)


def dot(a, b, ca, cb):
    return lax.dot_general(a, b, (((ca,), (cb,)), ((), ())), preferred_element_type=F32)


def params(limit):
    return pltpu.CompilerParams(vmem_limit_bytes=limit * MiB)


def spans(cuts):
    start = 0
    for size in cuts:
        yield pl.ds(start, size)
        start += size


def column_block_at(start, width):
    return pl.ds(pl.multiple_of(start, 128), width)


def column_block(index, width):
    return pl.ds(pl.multiple_of(index * width, 128), width)


def project_kernel(cuts, inner, gradient, feedback, basis, *refs):
    merged, mine, other, p_buf, g_buf, f_buf, b_buf, g_sem, f_sem, b_sem = refs
    core = lax.axis_index("core")
    rank, cols = basis.shape
    fetch_basis = pltpu.make_async_copy(basis, b_buf, b_sem)
    fetch_basis.start()
    fetch = []
    for i, part in enumerate(spans(cuts)):
        pair = (
            pltpu.make_async_copy(feedback.at[part], f_buf.at[part], f_sem.at[i]),
            pltpu.make_async_copy(gradient.at[part], g_buf.at[part], g_sem.at[i]),
        )
        for copy in pair:
            copy.start()
        fetch.append(pair)
    fetch_basis.wait()
    w_high, w_low = halves(b_buf[...])
    stack = jnp.concatenate([w_high, w_low], axis=0)
    terms = []
    for i, part in enumerate(spans(cuts)):
        for copy in fetch[i]:
            copy.wait()
        total = None
        for at in range(0, cols, inner):
            span = pl.ds(at, inner)
            value = g_buf[part, span].astype(F32) + f_buf[part, span]
            merged[part, span] = value
            high, low = halves(value)
            both = dot(high, stack[:, at : at + inner], 1, 1)
            term = both[:, :rank] + both[:, rank:]
            term = term + dot(low, w_high[:, at : at + inner], 1, 1)
            total = term if total is None else total + term
        terms.append(total)
    p_buf[...] = jnp.concatenate(terms, axis=0).T
    half = rank // 2
    mine[...] = p_buf[pl.ds(pl.multiple_of(core * half, 8), half)]
    other[...] = p_buf[pl.ds(pl.multiple_of((1 - core) * half, 8), half)]


def project(gradient, feedback, basis, cuts=(128, 128), inner=512):
    rows, cols = feedback.shape
    rank = basis.shape[0]
    arrays = [
        pltpu.with_memory_space_constraint(x, pltpu.HBM)
        for x in (gradient, feedback, basis)
    ]
    return pl.pallas_call(
        functools.partial(project_kernel, cuts, inner),
        in_specs=[HBM] * 3,
        out_specs=[VMEM] * 3,
        out_shape=[pltpu.VMEM((rows, cols), F32)]
        + [pltpu.VMEM((rank // 2, rows), F32)] * 2,
        scratch_shapes=[
            pltpu.VMEM((rank, rows), F32),
            pltpu.VMEM((rows, cols), BF16),
            pltpu.VMEM((rows, cols), F32),
            pltpu.VMEM((rank, cols), F32),
            pltpu.SemaphoreType.DMA((len(cuts),)),
            pltpu.SemaphoreType.DMA((len(cuts),)),
            pltpu.SemaphoreType.DMA,
        ],
        compiler_params=params(20),
        name="project",
    )(*arrays)


def factor_kernel(blocks, projected, merged, out):
    rank = projected.shape[0]
    count, depth, width = out.shape
    groups = count // blocks
    p_high, p_low = halves(projected[...])
    stack = jnp.concatenate([p_high, p_low], axis=0)
    for k in range(blocks):
        high, low = halves(merged[:, k * width : (k + 1) * width])
        both = dot(stack, high, 1, 0)
        term = both[:rank] + both[rank:] + dot(p_high, low, 1, 0)
        out[k * groups : (k + 1) * groups] = term.reshape(groups, depth, width)


def partial_factor(projected, merged, blocks, shape):
    merged = pltpu.with_memory_space_constraint(merged, pltpu.VMEM)
    return pl.pallas_call(
        functools.partial(factor_kernel, blocks),
        in_specs=[VMEM] * 2,
        out_specs=VMEM,
        out_shape=jax.ShapeDtypeStruct(shape, F32),
        compiler_params=params(8),
        name="partial_factor",
    )(projected, merged)


def rebuild_kernel(scale, across, count, basis, merged, factor, *refs):
    approx, updated, a_buf, u_buf, a_sem, u_sem = refs[-6:]
    rank = basis.shape[1] // 3
    groups, _, width = factor.shape
    groups //= count
    place = lax.axis_index("yh")
    place = 1 - place if across else place
    left = basis[...]
    copies = []
    for i in range(count):
        f = factor[i * groups : (i + 1) * groups].reshape(rank, width)
        f_high, f_low = halves(f)
        right = jnp.concatenate([f_high, f_low, f_high], axis=0)
        start = (2 * place + i) * width
        for j, (at, size) in enumerate(((0, 384), (384, 512))):
            value = dot(left, right[:, at : at + size], 1, 0)
            part = column_block_at(start + at, size)
            a_buf[i, :, at : at + size] = value.astype(BF16)
            u_buf[i, :, at : at + size] = merged[:, part] - value * scale
            for buf, out, sem in ((u_buf, updated, u_sem), (a_buf, approx, a_sem)):
                copy = pltpu.make_async_copy(buf.at[i, :, pl.ds(at, size)], out.at[:, part], sem.at[2 * i + j])
                copy.start()
                copies.append(copy)
    for copy in copies:
        copy.wait()


def rebuild(basis, merged, factor, across, replicas, earlier=()):
    rows, cols = merged.shape
    width = factor.shape[2]
    count = cols // width // 2
    merged = pltpu.with_memory_space_constraint(merged, pltpu.VMEM)
    earlier = [pltpu.with_memory_space_constraint(x, pltpu.HBM) for x in earlier]
    return pl.pallas_call(
        functools.partial(rebuild_kernel, 1.0 / replicas, across, count),
        in_specs=[VMEM] * 3 + [HBM] * len(earlier),
        out_specs=[HBM] * 2,
        out_shape=[pltpu.HBM((rows, cols), BF16), pltpu.HBM((rows, cols), F32)],
        input_output_aliases={3 + i: i for i in range(len(earlier))},
        scratch_shapes=[
            pltpu.VMEM((count, rows, width), BF16),
            pltpu.VMEM((count, rows, width), F32),
            pltpu.SemaphoreType.DMA((2 * count,)),
            pltpu.SemaphoreType.DMA((2 * count,)),
        ],
        compiler_params=params(20),
        name="rebuild",
    )(basis, merged, factor, *earlier)


def solve_kernel(w, projected_ref, out_ref):
    p = projected_ref[...]
    rank = p.shape[0]
    exact = functools.partial(
        lax.dot_general, precision=lax.Precision.HIGHEST, preferred_element_type=F32
    )
    gram = exact(p, p, (((1,), (1,)), ((), ())))
    eye = (
        lax.broadcasted_iota(jnp.int32, (rank, rank), 0)
        == lax.broadcasted_iota(jnp.int32, (rank, rank), 1)
    ).astype(F32)
    state = jnp.concatenate([gram, eye], axis=1)
    row_id = lax.broadcasted_iota(jnp.int32, (rank, 1), 0)
    inverse_pivots = jnp.zeros((rank, 2 * rank), F32)
    for k in range(0, rank, w):
        rows = [state[k + j : k + j + 1, :] for j in range(w)]
        cols = [jnp.broadcast_to(state[:, k + j : k + j + 1], state.shape) for j in range(w)]
        block = {(i, j): cols[j][k + i : k + i + 1, :] for i in range(w) for j in range(i + 1)}
        change = None
        inverse, ratio = [], {}
        for j in range(w):
            inverse.append(1.0 / block[j, j])
            for i in range(j + 1, w):
                ratio[i, j] = block[i, j] * inverse[j]
            for i in range(j + 1, w):
                for l in range(j + 1, i + 1):
                    block[i, l] = block[i, l] - ratio[i, j] * block[l, j]
        for j in range(w):
            for i in range(j + 1, w):
                rows[i] = rows[i] - ratio[i, j] * rows[j]
                cols[i] = cols[i] - ratio[i, j] * cols[j]
            inverse_pivots = jnp.where(row_id == k + j, inverse[j], inverse_pivots)
            if k + j + 1 < rank:
                term = jnp.where(row_id > k + j, cols[j] * inverse[j], 0.0) * rows[j]
                change = term if change is None else change + term
        if change is not None:
            state = state - change
    unit = state[:, rank:]
    basis = exact(unit, p, (((1,), (0,)), ((), ()))) * inverse_pivots[:, :1]
    high, low = halves(exact(unit, basis, (((0,), (0,)), ((), ()))))
    out_ref[...] = jnp.concatenate([high, high, low], axis=0).T


def solve(projected):
    return pl.pallas_call(
        functools.partial(solve_kernel, 8),
        out_shape=jax.ShapeDtypeStruct((projected.shape[1], 3 * projected.shape[0]), BF16),
        compiler_params=params(4),
        name="solve",
    )(projected)


def rotate(x, axis, size, step):
    return lax.ppermute(x, axis, [(i, (i + step) % size) for i in range(size)])


def mirror(x, size):
    pairs = [(i, size - 1 - i) for i in range(size)]
    return lax.ppermute(x, ("yh", "yl"), pairs)


def spread(x, axes, size):
    return lax.all_to_all(jnp.broadcast_to(x[None], (size,) + x.shape), axes, 0, 0)


def added(stacked):
    return functools.reduce(jnp.add, [stacked[i] for i in range(stacked.shape[0])])


def local(sizes, gradient, feedback, warm_basis):
    z, x = sizes["z"], sizes["x"]
    y = sizes["yh"] * sizes["yl"]
    rank, cols = warm_basis.shape
    width = cols // y
    merged, mine, other = project(gradient[0], feedback[0], warm_basis)

    mine = mine + rotate(other, "core", 2, 1)
    mine = added(spread(mine, ("yh", "yl", "x"), y * x))
    mine = added(spread(mine, "z", z))
    projected = jnp.concatenate([mine, rotate(mine, "core", 2, 1)])

    factor = partial_factor(projected, merged, y, (y * z, rank // z, width))
    summed = added(lax.all_to_all(factor, ("yh", "yl", "z"), 0, 0))
    here = spread(summed, ("yl", "z"), y // 2 * z)
    there = mirror(here, y)
    basis = solve(projected)
    build = functools.partial(rebuild, basis, merged, replicas=y * z)
    outs = build(here, False)
    approx, updated = build(there, True, earlier=outs)
    return (approx, updated[None])


def solution(mesh):
    sizes = {"yh": 2, "yl": 2, "z": 8, "x": 4, "core": 2}
    inner = Mesh(mesh.devices.reshape(tuple(sizes.values())), tuple(sizes))
    dp, mp = ("yh", "yl", "z"), ("x", "core")
    return jax.shard_map(
        functools.partial(local, sizes),
        mesh=inner,
        in_specs=(P(dp, None, mp), P(dp, None, mp), P(None, mp)),
        out_specs=(P(None, mp), P(dp, None, mp)),
        check_vma=False,
    )
```

```python
import functools

import jax
import jax.numpy as jnp
from jax import lax
from jax.experimental import pallas as pl
from jax.experimental.pallas import tpu as pltpu
from jax.sharding import Mesh
from jax.sharding import PartitionSpec as P

F32 = jnp.float32
BF16 = jnp.bfloat16
MiB = 1024 * 1024
VMEM = pl.BlockSpec(memory_space=pltpu.VMEM)
HBM = pl.BlockSpec(memory_space=pltpu.HBM)


def halves(value):
    high = value.astype(BF16)
    return high, (value - high.astype(F32)).astype(BF16)


def dot(a, b, ca, cb):
    return lax.dot_general(a, b, (((ca,), (cb,)), ((), ())), preferred_element_type=F32)


def params(limit):
    return pltpu.CompilerParams(vmem_limit_bytes=limit * MiB)


def spans(cuts):
    start = 0
    for size in cuts:
        yield pl.ds(start, size)
        start += size


def column_block_at(start, width):
    return pl.ds(pl.multiple_of(start, 128), width)


def column_block(index, width):
    return pl.ds(pl.multiple_of(index * width, 128), width)


def project_kernel(cuts, inner, gradient, feedback, basis, *refs):
    merged, mine, other, p_buf, g_buf, f_buf, b_buf, g_sem, f_sem, b_sem = refs
    core = lax.axis_index("core")
    rank, cols = basis.shape
    fetch_basis = pltpu.make_async_copy(basis, b_buf, b_sem)
    fetch_basis.start()
    fetch = []
    for i, part in enumerate(spans(cuts)):
        pair = (
            pltpu.make_async_copy(feedback.at[part], f_buf.at[part], f_sem.at[i]),
            pltpu.make_async_copy(gradient.at[part], g_buf.at[part], g_sem.at[i]),
        )
        for copy in pair:
            copy.start()
        fetch.append(pair)
    fetch_basis.wait()
    w_high, w_low = halves(b_buf[...])
    stack = jnp.concatenate([w_high, w_low], axis=0)
    for i, part in enumerate(spans(cuts)):
        for copy in fetch[i]:
            copy.wait()
        total = None
        for at in range(0, cols, inner):
            span = pl.ds(at, inner)
            value = g_buf[part, span].astype(F32) + f_buf[part, span]
            merged[part, span] = value
            high, low = halves(value)
            both = dot(high, stack[:, at : at + inner], 1, 1)
            term = both[:, :rank] + both[:, rank:]
            term = term + dot(low, w_high[:, at : at + inner], 1, 1)
            total = term if total is None else total + term
        p_buf[:, part] = total.T
    half = rank // 2
    mine[...] = p_buf[pl.ds(pl.multiple_of(core * half, 8), half)]
    other[...] = p_buf[pl.ds(pl.multiple_of((1 - core) * half, 8), half)]


def project(gradient, feedback, basis, cuts=(128, 128), inner=512):
    rows, cols = feedback.shape
    rank = basis.shape[0]
    arrays = [
        pltpu.with_memory_space_constraint(x, pltpu.HBM)
        for x in (gradient, feedback, basis)
    ]
    return pl.pallas_call(
        functools.partial(project_kernel, cuts, inner),
        in_specs=[HBM] * 3,
        out_specs=[VMEM] * 3,
        out_shape=[pltpu.VMEM((rows, cols), F32)]
        + [pltpu.VMEM((rank // 2, rows), F32)] * 2,
        scratch_shapes=[
            pltpu.VMEM((rank, rows), F32),
            pltpu.VMEM((rows, cols), BF16),
            pltpu.VMEM((rows, cols), F32),
            pltpu.VMEM((rank, cols), F32),
            pltpu.SemaphoreType.DMA((len(cuts),)),
            pltpu.SemaphoreType.DMA((len(cuts),)),
            pltpu.SemaphoreType.DMA,
        ],
        compiler_params=params(20),
        name="project",
    )(*arrays)


def factor_kernel(blocks, projected, merged, out):
    rank = projected.shape[0]
    count, depth, width = out.shape
    groups = count // blocks
    p_high, p_low = halves(projected[...])
    stack = jnp.concatenate([p_high, p_low], axis=0)
    for k in range(blocks):
        high, low = halves(merged[:, k * width : (k + 1) * width])
        both = dot(stack, high, 1, 0)
        term = both[:rank] + both[rank:] + dot(p_high, low, 1, 0)
        out[k * groups : (k + 1) * groups] = term.reshape(groups, depth, width)


def partial_factor(projected, merged, blocks, shape):
    merged = pltpu.with_memory_space_constraint(merged, pltpu.VMEM)
    return pl.pallas_call(
        functools.partial(factor_kernel, blocks),
        in_specs=[VMEM] * 2,
        out_specs=VMEM,
        out_shape=jax.ShapeDtypeStruct(shape, F32),
        compiler_params=params(8),
        name="partial_factor",
    )(projected, merged)


def rebuild_kernel(scale, across, count, basis, merged, factor, *refs):
    approx, updated, a_buf, u_buf, a_sem, u_sem = refs[-6:]
    rank = basis.shape[1] // 3
    groups, _, width = factor.shape
    groups //= count
    place = lax.axis_index("yh")
    place = 1 - place if across else place
    left = basis[...]
    copies = []
    for i in range(count):
        f = factor[i * groups : (i + 1) * groups].reshape(rank, width)
        f_high, f_low = halves(f)
        right = jnp.concatenate([f_high, f_low, f_high], axis=0)
        start = (2 * place + i) * width
        for j, (at, size) in enumerate(((0, 384), (384, 512))):
            value = dot(left, right[:, at : at + size], 1, 0)
            part = column_block_at(start + at, size)
            a_buf[i, :, at : at + size] = value.astype(BF16)
            u_buf[i, :, at : at + size] = merged[:, part] - value * scale
            for buf, out, sem in ((u_buf, updated, u_sem), (a_buf, approx, a_sem)):
                copy = pltpu.make_async_copy(buf.at[i, :, pl.ds(at, size)], out.at[:, part], sem.at[2 * i + j])
                copy.start()
                copies.append(copy)
    for copy in copies:
        copy.wait()


def rebuild(basis, merged, factor, across, replicas, earlier=()):
    rows, cols = merged.shape
    width = factor.shape[2]
    count = cols // width // 2
    merged = pltpu.with_memory_space_constraint(merged, pltpu.VMEM)
    earlier = [pltpu.with_memory_space_constraint(x, pltpu.HBM) for x in earlier]
    return pl.pallas_call(
        functools.partial(rebuild_kernel, 1.0 / replicas, across, count),
        in_specs=[VMEM] * 3 + [HBM] * len(earlier),
        out_specs=[HBM] * 2,
        out_shape=[pltpu.HBM((rows, cols), BF16), pltpu.HBM((rows, cols), F32)],
        input_output_aliases={3 + i: i for i in range(len(earlier))},
        scratch_shapes=[
            pltpu.VMEM((count, rows, width), BF16),
            pltpu.VMEM((count, rows, width), F32),
            pltpu.SemaphoreType.DMA((2 * count,)),
            pltpu.SemaphoreType.DMA((2 * count,)),
        ],
        compiler_params=params(20),
        name="rebuild",
    )(basis, merged, factor, *earlier)


def solve_kernel(w, projected_ref, out_ref):
    p = projected_ref[...]
    rank = p.shape[0]
    exact = functools.partial(
        lax.dot_general, precision=lax.Precision.HIGHEST, preferred_element_type=F32
    )
    gram = exact(p, p, (((1,), (1,)), ((), ())))
    eye = (
        lax.broadcasted_iota(jnp.int32, (rank, rank), 0)
        == lax.broadcasted_iota(jnp.int32, (rank, rank), 1)
    ).astype(F32)
    state = jnp.concatenate([gram, eye], axis=1)
    row_id = lax.broadcasted_iota(jnp.int32, (rank, 1), 0)
    inverse_pivots = jnp.zeros((rank, 2 * rank), F32)
    for k in range(0, rank, w):
        rows = [state[k + j : k + j + 1, :] for j in range(w)]
        cols = [jnp.broadcast_to(state[:, k + j : k + j + 1], state.shape) for j in range(w)]
        block = {(i, j): cols[j][k + i : k + i + 1, :] for i in range(w) for j in range(i + 1)}
        change = None
        inverse, ratio = [], {}
        for j in range(w):
            inverse.append(1.0 / block[j, j])
            for i in range(j + 1, w):
                ratio[i, j] = block[i, j] * inverse[j]
            for i in range(j + 1, w):
                for l in range(j + 1, i + 1):
                    block[i, l] = block[i, l] - ratio[i, j] * block[l, j]
        for j in range(w):
            for i in range(j + 1, w):
                rows[i] = rows[i] - ratio[i, j] * rows[j]
                cols[i] = cols[i] - ratio[i, j] * cols[j]
            inverse_pivots = jnp.where(row_id == k + j, inverse[j], inverse_pivots)
            if k + j + 1 < rank:
                term = jnp.where(row_id > k + j, cols[j] * inverse[j], 0.0) * rows[j]
                change = term if change is None else change + term
        if change is not None:
            state = state - change
    unit = state[:, rank:]
    basis = exact(unit, p, (((1,), (0,)), ((), ()))) * inverse_pivots[:, :1]
    high, low = halves(exact(unit, basis, (((0,), (0,)), ((), ()))))
    out_ref[...] = jnp.concatenate([high, high, low], axis=0).T


def solve(projected):
    return pl.pallas_call(
        functools.partial(solve_kernel, 8),
        out_shape=jax.ShapeDtypeStruct((projected.shape[1], 3 * projected.shape[0]), BF16),
        compiler_params=params(4),
        name="solve",
    )(projected)


def rotate(x, axis, size, step):
    return lax.ppermute(x, axis, [(i, (i + step) % size) for i in range(size)])


def mirror(x, size):
    pairs = [(i, size - 1 - i) for i in range(size)]
    return lax.ppermute(x, ("yh", "yl"), pairs)


def spread(x, axes, size):
    return lax.all_to_all(jnp.broadcast_to(x[None], (size,) + x.shape), axes, 0, 0)


def added(stacked):
    return functools.reduce(jnp.add, [stacked[i] for i in range(stacked.shape[0])])


def local(sizes, gradient, feedback, warm_basis):
    z, x = sizes["z"], sizes["x"]
    y = sizes["yh"] * sizes["yl"]
    rank, cols = warm_basis.shape
    width = cols // y
    merged, mine, other = project(gradient[0], feedback[0], warm_basis)

    mine = mine + rotate(other, "core", 2, 1)
    mine = added(spread(mine, ("yh", "yl", "x"), y * x))
    mine = added(spread(mine, "z", z))
    projected = jnp.concatenate([mine, rotate(mine, "core", 2, 1)])

    factor = partial_factor(projected, merged, y, (y * z, rank // z, width))
    summed = added(lax.all_to_all(factor, ("yh", "yl", "z"), 0, 0))
    here = spread(summed, ("yl", "z"), y // 2 * z)
    there = mirror(here, y)
    basis = solve(projected)
    build = functools.partial(rebuild, basis, merged, replicas=y * z)
    outs = build(here, False)
    approx, updated = build(there, True, earlier=outs)
    return (approx, updated[None])


def solution(mesh):
    sizes = {"yh": 2, "yl": 2, "z": 8, "x": 4, "core": 2}
    inner = Mesh(mesh.devices.reshape(tuple(sizes.values())), tuple(sizes))
    dp, mp = ("yh", "yl", "z"), ("x", "core")
    return jax.shard_map(
        functools.partial(local, sizes),
        mesh=inner,
        in_specs=(P(dp, None, mp), P(dp, None, mp), P(None, mp)),
        out_specs=(P(None, mp), P(dp, None, mp)),
        check_vma=False,
    )
```
